128 devices in a mesh: head: 4 (over y_hi, core), blk: 32 (over z, y_lo, x).
Axes of the slice: x: 4, y: 4 (y_hi: 2, y_lo: 2; y = y_hi * 2 + y_lo), z: 4, core: 2. Of those that a mesh axis runs over, the one named last changes fastest.
Arguments:
- queries: bfloat16 [32768, 1536], P(('blk', 'head')), may hold values from -24 to 24
- key_rows: bfloat16 [32768, 1536], P(('blk', 'head')), may hold values from -6 to 6
- value_rows: bfloat16 [32768, 1536], P(('blk', 'head')), may hold values from -6 to 6
- tile_lists: int32 [256, 16], P('blk'), may hold values from 0 to 255, as said below
Outputs:
- attended: bfloat16 [32768, 1536], P(('blk', 'head'))
The draws below stay inside these ranges and needn't reach their ends.
Inputs may be any that keep to these rules, and one draw needn't show every extreme that they name: `tile_lists`: tile index (f * 2 + i) * 2 + j is frame tile f, height tile i, width tile j. Row t holds 16 distinct tiles whose frame tile lies within 4 of that of tile t, distances counted cyclically over the clip's frame tiles, and t itself among them.
All inputs are finite; a program needn't handle non-finite values.
Results may differ from the reference program's by a relative error of at most 0.0085.
Values may be sent and summed in bfloat16 or wider, within the bound.
A program may use at most 128 MiB of HBM per device.

```python
import jax
import jax.numpy as jnp
from jax import lax

HEADS = 12
HD = 128
TILE = 128
TH = 2
TW = 2
SEL = 16
TOKENS = 32768
NT = 256
RF = 4


def draw_queries(key, part):
    key = jax.random.fold_in(key, 3)
    return jnp.clip(jax.random.normal(key, (TOKENS, HEADS * HD), jnp.float32), -6.0, 6.0).astype(jnp.bfloat16)


def draw_key_rows(key, part):
    key = jax.random.fold_in(key, 5)
    return jnp.clip(jax.random.normal(key, (TOKENS, HEADS * HD), jnp.float32), -6.0, 6.0).astype(jnp.bfloat16)


def draw_tile_lists(key, part):
    key = jax.random.fold_in(key, 7)
    spots = TH * TW
    frames = NT // spots
    span = (2 * RF + 1) * spots
    tiles = jnp.arange(NT, dtype=jnp.int32)[:, None]
    frame = tiles // spots
    option = jnp.arange(span, dtype=jnp.int32)[None, :]
    target_frame = (frame + option // spots - RF + frames) % frames
    target = target_frame * spots + option % spots
    noise = jax.random.randint(key, (NT, span), 0, 2 ** 20, dtype=jnp.int32)
    score = noise * span + option
    score = score + jnp.where(target == tiles, 2 ** 28, 0)
    unused, picked = lax.top_k(score, SEL)
    return jnp.take_along_axis(target, picked, axis=1).astype(jnp.int32)


def shard_levels(stream_key, extent, split, smallest, largest):
    level = 1.0
    for position, parts in split:
        steps = jax.random.uniform(jax.random.fold_in(jax.random.fold_in(stream_key, 6), position), (parts,), jnp.float32, smallest / len(split), largest / len(split))
        level = level * jnp.repeat(jnp.exp(steps), extent[position] // parts).reshape((-1,) + (1,) * (len(extent) - 1 - position))
    return level


def centred(stream_key, shape, deviation, bound, split=(), kind=jnp.bfloat16):
    loudness = shard_levels(stream_key, shape, split, -0.22, 0.18) if split else 1.0
    entries = jax.random.normal(stream_key, shape, jnp.float32) * deviation * loudness
    return jnp.minimum(jnp.maximum(entries, -bound), bound).astype(kind)


def setup_inputs(seed: int = 0) -> dict:
    key_list = jax.random.split(jax.random.key(seed), 5)
    queries = draw_queries(jax.random.fold_in(key_list[4], 71), 0)
    key_rows = draw_key_rows(jax.random.fold_in(key_list[4], 71), 0)
    value_rows = centred(key_list[2], (TOKENS, HEADS * HD), 1.0, 6.0, ((0, 128),))
    tile_lists = draw_tile_lists(jax.random.fold_in(key_list[4], 71), 0)
    return {"queries": queries, "key_rows": key_rows, "value_rows": value_rows, "tile_lists": tile_lists}


def reference(queries, key_rows, value_rows, tile_lists):
    query_tiles = queries.reshape(NT, TILE, HEADS, HD)
    key_tiles = key_rows.reshape(NT, TILE, HEADS, HD)
    value_tiles = value_rows.reshape(NT, TILE, HEADS, HD)

    def one_tile(item):
        query_tile, chosen = item
        keys = key_tiles[chosen].reshape(SEL * TILE, HEADS, HD).astype(jnp.float32)
        values = value_tiles[chosen].reshape(SEL * TILE, HEADS, HD).astype(jnp.float32)
        scores = jnp.einsum("qhd,khd->hqk", query_tile.astype(jnp.float32), keys) * (HD ** -0.5)
        peak = jnp.max(scores, axis=2, keepdims=True)
        weights = jnp.exp(scores - peak)
        total = jnp.sum(weights, axis=2)
        rounded = lax.optimization_barrier(weights.astype(jnp.bfloat16)).astype(jnp.float32)
        mixed = jnp.einsum("hqk,khd->qhd", rounded, values)
        mixed = mixed / jnp.transpose(total)[:, :, None]
        return mixed.astype(jnp.bfloat16).reshape(TILE, HEADS * HD)

    result = lax.map(one_tile, (query_tiles, tile_lists))
    return result.reshape(TOKENS, HEADS * HD)
```

```python
import functools

import jax
import jax.numpy as jnp
from jax import lax
from jax.experimental import pallas as pl
from jax.experimental.pallas import tpu as pltpu
from jax.sharding import PartitionSpec as P

MESH = pl.DeviceIdType.MESH
HD = 128
TILE = 128
SEL = 16
GROUP = 3 * HD
ROW = 32
HALO = ROW // 2
EXP2 = HD ** -0.5 * 1.4426950408889634


def kernel(q_hbm, k_hbm, v_hbm, lists_hbm, out_hbm, relay_k, relay_v, relay_q, relay_o, win_k, win_v, win_q, win_o,
           lists_r, lists_v, lists_s, xs, xr, ys, yr, fs, fr, ls, lxr, lyr, lc, oys, oyr, oxs, oxr):
    head, blk = lax.axis_index("head"), lax.axis_index("blk")
    x, y_lo, z = blk % 4, (blk // 4) % 2, blk // 8
    core = head % 2
    y = (head // 2) * 2 + y_lo
    mine = (y + 7 - x) % 4
    active = mine < 3
    own_row = core == y_lo

    def device(dx, dy, dz, dc):
        return {"head": (dy // 2) * 2 + dc, "blk": dz * 8 + (dy % 2) * 4 + dx}

    def remote(src, dst, send, recv, to):
        return pltpu.make_async_remote_copy(
            src_ref=src, dst_ref=dst, send_sem=send, recv_sem=recv, device_id=to, device_id_type=MESH
        )

    def wait(ref, sem):
        pltpu.make_async_copy(ref, ref, sem).wait()

    def either(local, src, dst, send, recv, to):
        @pl.when(local)
        def _():
            pltpu.make_async_copy(src, dst, recv).start()

        @pl.when(jnp.logical_not(local))
        def _():
            remote(src, dst, send, recv, to).start()

    barrier = pltpu.get_barrier_semaphore()
    for d in range(1, 4):
        pl.semaphore_signal(barrier, inc=1, device_id=device((x + d) % 4, y, z, core), device_id_type=MESH)
        for c in range(2):
            pl.semaphore_signal(barrier, inc=1, device_id=device(x, (y + d) % 4, z, c), device_id_type=MESH)
    pl.semaphore_signal(barrier, inc=1, device_id=device(x, y, z, 1 - core), device_id_type=MESH)
    across = device(x, y, (z + 2 * core + 3) % 4, 1 - core)
    pl.semaphore_signal(barrier, inc=1, device_id=across, device_id_type=MESH)
    pl.semaphore_wait(barrier, 11)

    arrays = ((k_hbm, relay_k, win_k, HALO), (v_hbm, relay_v, win_v, HALO), (q_hbm, relay_q, win_q, 0))

    def along_x(a):
        src, relay = arrays[a][:2]
        for d in (2, 1, 3):
            to = (x + d) % 4
            columns = pl.ds(pl.multiple_of(to * GROUP, GROUP), GROUP)
            remote(src.at[:, :, columns], relay.at[x], xs.at[a], xr.at[a, d], device(to, y, z, core)).start()

    def along_y(a, d):
        src, relay, window, base = arrays[a]
        start = (x + 4 - d) % 4
        if d:
            wait(relay.at[start], xr.at[a, d])

        def one(j, carry):
            to = (x + 1 + j) % 4
            if d:
                block = relay.at[start, :, :, pl.ds(pl.multiple_of(j * HD, HD), HD)]
            else:
                block = src.at[:, :, pl.ds(pl.multiple_of((3 * x + j) * HD, HD), HD)]
            place = window.at[pl.ds(base + start * 8 + head * 2, 2)]
            either(own_row & (to == y), block, place, ys.at[a], yr.at[a, start], device(x, to, z, y_lo))
            return carry

        lax.fori_loop(0, 3, one, 0)

    before = device(x, y, (z + 3 + core) % 4, 1 - core)
    after = device(x, y, (z + core) % 4, 1 - core)

    def forward(a, d):
        window = arrays[a][2]
        start = (x + 4 - d) % 4
        block = window.at[pl.ds(HALO + start * 8, 8)]
        wait(block, yr.at[a, start])

        @pl.when(start < 2)
        def _():
            place = window.at[pl.ds(HALO + ROW + start * 8, 8)]
            remote(block, place, fs.at[a], fr.at[a, 1], before).start()

        @pl.when(start >= 2)
        def _():
            place = window.at[pl.ds((start - 2) * 8, 8)]
            remote(block, place, fs.at[a], fr.at[a, 0], after).start()

    for d in range(1, 4):
        remote(lists_hbm, lists_r.at[x], ls, lxr.at[d], device((x + d) % 4, y, z, core)).start()
    own_lists = pltpu.make_async_copy(lists_hbm, lists_r.at[x], lc.at[0])
    own_lists.start()

    along_x(0)
    along_y(0, 0)
    along_x(1)
    along_y(1, 0)
    along_x(2)
    along_y(2, 0)

    own_lists.wait()
    for d in range(1, 4):
        wait(lists_r.at[x], lxr.at[d])

    @pl.when(head == 0)
    def _():
        for j in range(3):
            to = (x + 1 + j) % 4
            either(own_row & (to == y), lists_r, lists_v, ls, lyr, device(x, to, z, y_lo))

    for d in range(1, 4):
        along_y(0, d)

    @pl.when(active)
    def _():
        forward(0, 0)
        for d in range(1, 4):
            forward(0, d)

    for d in range(1, 4):
        along_y(1, d)

    @pl.when(active)
    def _():
        for d in range(4):
            forward(1, d)

    for d in range(1, 4):
        along_y(2, d)

    def out_x(d):
        to = (x + 4 - d) % 4
        wait(relay_o.at[to], oyr.at[d])
        columns = pl.ds(pl.multiple_of(x * GROUP, GROUP), GROUP)
        remote(relay_o.at[to], out_hbm.at[:, :, columns], oxs, oxr, device(to, y, z, core)).start()

    @pl.when(active)
    def _():
        wait(lists_v, lyr)
        to_scalar = pltpu.make_async_copy(lists_v, lists_s, lc.at[1])
        to_scalar.start()
        for a in range(2):
            for side in range(2):
                wait(win_k.at[pl.ds(0, HALO)], fr.at[a, side])
        to_scalar.wait()

        def attend(start, peer):
            for t in range(2):
                row = start * 8 + peer * 2 + t
                spots = [lists_s[start, peer * 2 + t, e] for e in range(SEL)]
                keys = jnp.concatenate([win_k[w] for w in spots], axis=0)
                scores = lax.dot_general(
                    win_q[row], keys, (((1,), (1,)), ((), ())), preferred_element_type=jnp.float32
                )
                peak = jnp.max(scores, axis=1, keepdims=True)
                weights = jnp.exp2((scores - peak) * EXP2)
                total = jnp.sum(weights, axis=1, keepdims=True)
                values = jnp.concatenate([win_v[w] for w in spots], axis=0)
                mixed = jnp.dot(weights.astype(jnp.bfloat16), values, preferred_element_type=jnp.float32)
                win_o[row] = (mixed / total).astype(jnp.bfloat16)

        for d in range(4):
            start = (x + 4 - d) % 4
            wait(win_q.at[pl.ds(start * 8, 8)], yr.at[2, start])

            def slot(peer, carry):
                attend(start, peer)
                block = win_o.at[pl.ds(start * 8 + peer * 2, 2)]
                to = {"head": peer, "blk": z * 8 + core * 4 + x}
                local = own_row & (peer == head)
                if d:
                    place = relay_o.at[start, :, :, pl.ds(pl.multiple_of(mine * HD, HD), HD)]
                    either(local, block, place, oys, oyr.at[d], to)
                else:
                    place = out_hbm.at[:, :, pl.ds(pl.multiple_of((3 * x + mine) * HD, HD), HD)]
                    either(local, block, place, oys, oxr, to)
                return carry

            lax.fori_loop(0, 4, slot, 0)
            if d >= 2:
                out_x(d - 1)
        out_x(3)

    @pl.when(jnp.logical_not(active))
    def _():
        for d in range(1, 4):
            out_x(d)

    wait(out_hbm, oxr)
    wait(relay_o.at[pl.ds(0, 3)], oxs)
    for d in range(3):
        wait(lists_r.at[x], ls)
    for a in range(3):
        wait(relay_k.at[pl.ds(0, 3)], xs.at[a])
    itself = own_row & active

    @pl.when(itself)
    def _():
        for a in range(3):
            wait(win_q.at[pl.ds(0, 16)], ys.at[a])
        wait(win_q.at[pl.ds(0, 24)], oys)

    @pl.when(jnp.logical_not(itself))
    def _():
        for a in range(3):
            wait(win_q.at[pl.ds(0, 24)], ys.at[a])

    @pl.when(active & jnp.logical_not(own_row))
    def _():
        wait(win_q, oys)

    @pl.when(active)
    def _():
        for a in range(2):
            wait(win_q, fs.at[a])

    @pl.when(head == 0)
    def _():
        for j in range(2):
            wait(lists_v, ls)

        @pl.when(jnp.logical_not(itself))
        def _():
            wait(lists_v, ls)


def local(queries, key_rows, value_rows, tile_lists):
    bf16, dma = jnp.bfloat16, pltpu.SemaphoreType.DMA
    relay = pltpu.VMEM((4, 2, TILE, GROUP), bf16)
    spots = (tile_lists + (256 + HALO - ROW * (lax.axis_index("blk") // 4))) % 256
    tiles = (2, TILE, queries.shape[1])
    result = pl.pallas_call(
        kernel,
        out_shape=jax.ShapeDtypeStruct(tiles, bf16),
        in_specs=[pl.BlockSpec(memory_space=pl.ANY)] * 4,
        out_specs=pl.BlockSpec(memory_space=pl.ANY),
        scratch_shapes=[
            relay, relay, relay, relay,
            pltpu.VMEM((2 * ROW, TILE, HD), bf16), pltpu.VMEM((2 * ROW, TILE, HD), bf16),
            pltpu.VMEM((ROW, TILE, HD), bf16), pltpu.VMEM((ROW, TILE, HD), bf16),
            pltpu.VMEM((4, 8, SEL), jnp.int32), pltpu.VMEM((4, 8, SEL), jnp.int32), pltpu.SMEM((4, 8, SEL), jnp.int32),
            dma((3,)), dma((3, 4)), dma((3,)), dma((3, 4)), dma((2,)), dma((2, 2)),
            dma, dma((4,)), dma, dma((2,)), dma, dma((4,)), dma, dma,
        ],
        compiler_params=pltpu.CompilerParams(collective_id=0, has_side_effects=True, vmem_limit_bytes=56 * 2**20),
        cost_estimate=pl.CostEstimate(flops=4 * 10**9, bytes_accessed=8 * 10**6, transcendentals=8 * 10**6),
    )(queries.reshape(tiles), key_rows.reshape(tiles), value_rows.reshape(tiles), spots)
    return result.reshape(queries.shape)


def solution(mesh):
    tokens = P(("blk", "head"), None)
    return jax.shard_map(
        local, mesh=mesh, in_specs=(tokens, tokens, tokens, P("blk", None)), out_specs=tokens, check_vma=False
    )
```

```python
import functools

import jax
import jax.numpy as jnp
from jax import lax
from jax.experimental import pallas as pl
from jax.experimental.pallas import tpu as pltpu
from jax.sharding import PartitionSpec as P

MESH = pl.DeviceIdType.MESH
HD = 128
TILE = 128
SEL = 16
GROUP = 3 * HD
ROW = 32
HALO = ROW // 2
EXP2 = HD ** -0.5 * 1.4426950408889634


def kernel(q_hbm, k_hbm, v_hbm, lists_hbm, out_hbm, relay_k, relay_v, relay_q, relay_o, win_k, win_v, win_q, win_o,
           lists_r, lists_v, lists_s, xs, xr, ys, yr, fs, fr, ls, lxr, lyr, lc, oys, oyr, oxs, oxr):
    head, blk = lax.axis_index("head"), lax.axis_index("blk")
    x, y_lo, z = blk % 4, (blk // 4) % 2, blk // 8
    core = head % 2
    y = (head // 2) * 2 + y_lo
    mine = (y + 7 - x) % 4
    active = mine < 3
    own_row = core == y_lo

    def device(dx, dy, dz, dc):
        return {"head": (dy // 2) * 2 + dc, "blk": dz * 8 + (dy % 2) * 4 + dx}

    def remote(src, dst, send, recv, to):
        return pltpu.make_async_remote_copy(
            src_ref=src, dst_ref=dst, send_sem=send, recv_sem=recv, device_id=to, device_id_type=MESH
        )

    def wait(ref, sem):
        pltpu.make_async_copy(ref, ref, sem).wait()

    def either(local, src, dst, send, recv, to):
        @pl.when(local)
        def _():
            pltpu.make_async_copy(src, dst, recv).start()

        @pl.when(jnp.logical_not(local))
        def _():
            remote(src, dst, send, recv, to).start()

    barrier = pltpu.get_barrier_semaphore()
    for d in range(1, 4):
        for c in range(2):
            pl.semaphore_signal(barrier, inc=1, device_id=device((x + d) % 4, y, z, c), device_id_type=MESH)
            pl.semaphore_signal(barrier, inc=1, device_id=device(x, (y + d) % 4, z, c), device_id_type=MESH)
    pl.semaphore_signal(barrier, inc=1, device_id=device(x, y, z, 1 - core), device_id_type=MESH)
    across = device(x, y, (z + 2 * core + 3) % 4, 1 - core)
    pl.semaphore_signal(barrier, inc=1, device_id=across, device_id_type=MESH)
    pl.semaphore_wait(barrier, 14)

    arrays = ((k_hbm, relay_k, win_k, HALO), (v_hbm, relay_v, win_v, HALO), (q_hbm, relay_q, win_q, 0))

    def along_x(a):
        src, relay = arrays[a][:2]
        for d in (2, 1, 3):
            to = (x + d) % 4
            columns = pl.ds(pl.multiple_of(to * GROUP, GROUP), GROUP)
            remote(src.at[:, :, columns], relay.at[x], xs.at[a], xr.at[a, d], device(to, y, z, core)).start()

    def along_y(a, d):
        src, relay, window, base = arrays[a]
        start = (x + 4 - d) % 4
        if d:
            wait(relay.at[start], xr.at[a, d])

        def one(j, carry):
            to = (x + 1 + j) % 4
            if d:
                block = relay.at[start, :, :, pl.ds(pl.multiple_of(j * HD, HD), HD)]
            else:
                block = src.at[:, :, pl.ds(pl.multiple_of((3 * x + j) * HD, HD), HD)]
            place = window.at[pl.ds(base + start * 8 + head * 2, 2)]
            either(own_row & (to == y), block, place, ys.at[a], yr.at[a, start], device(x, to, z, y_lo))
            return carry

        lax.fori_loop(0, 3, one, 0)

    def values_along_y():
        for d in (2, 1, 3):
            to = (y + d) % 4

            def one(k, carry):
                column = (to + 1 + k) % 4
                block = v_hbm.at[:, :, pl.ds(pl.multiple_of((3 * column + 2 - k) * HD, HD), HD)]
                remote(block, relay_v.at[y, k], xs.at[1], xr.at[1, d], device(x, to, z, core)).start()
                return carry

            lax.fori_loop(0, 3, one, 0)

    def values_along_x(d):
        source = (y + 4 - d) % 4
        if d:
            wait(relay_v.at[source, pl.ds(0, 3)], xr.at[1, d])

        def one(k, carry):
            to = (y + 1 + k) % 4
            if d:
                block = relay_v.at[source, k]
            else:
                block = v_hbm.at[:, :, pl.ds(pl.multiple_of((3 * to + 2 - k) * HD, HD), HD)]
            peer = (source // 2) * 2 + core
            place = win_v.at[pl.ds(HALO + x * 8 + peer * 2, 2)]
            local = (to == x) & (source % 2 == core)
            either(local, block, place, ys.at[1], yr.at[1, x], device(to, y, z, source % 2))
            return carry

        lax.fori_loop(0, 3, one, 0)

    before = device(x, y, (z + 3 + core) % 4, 1 - core)
    after = device(x, y, (z + core) % 4, 1 - core)

    def forward(a, d):
        window = arrays[a][2]
        start = (x + 4 - d) % 4
        block = window.at[pl.ds(HALO + start * 8, 8)]
        wait(block, yr.at[a, start])

        @pl.when(start < 2)
        def _():
            place = window.at[pl.ds(HALO + ROW + start * 8, 8)]
            remote(block, place, fs.at[a], fr.at[a, 1], before).start()

        @pl.when(start >= 2)
        def _():
            place = window.at[pl.ds((start - 2) * 8, 8)]
            remote(block, place, fs.at[a], fr.at[a, 0], after).start()

    for d in range(1, 4):
        remote(lists_hbm, lists_r.at[x], ls, lxr.at[d], device((x + d) % 4, y, z, core)).start()
    own_lists = pltpu.make_async_copy(lists_hbm, lists_r.at[x], lc.at[0])
    own_lists.start()

    along_x(0)
    values_along_y()
    along_y(0, 0)
    values_along_x(0)
    for d in (1, 3, 2):
        along_y(0, d)
        values_along_x(d)
    along_x(2)
    along_y(2, 0)

    own_lists.wait()
    for d in range(1, 4):
        wait(lists_r.at[x], lxr.at[d])

    @pl.when(head == 0)
    def _():
        for j in range(3):
            to = (x + 1 + j) % 4
            either(own_row & (to == y), lists_r, lists_v, ls, lyr, device(x, to, z, y_lo))

    @pl.when(active)
    def _():
        for a in range(2):
            for d in range(4):
                forward(a, d)

    for d in (1, 3, 2):
        along_y(2, d)

    def out_x(d):
        to = (x + 4 - d) % 4
        wait(relay_o.at[to], oyr.at[d])
        columns = pl.ds(pl.multiple_of(x * GROUP, GROUP), GROUP)
        remote(relay_o.at[to], out_hbm.at[:, :, columns], oxs, oxr, device(to, y, z, core)).start()

    @pl.when(active)
    def _():
        wait(lists_v, lyr)
        to_scalar = pltpu.make_async_copy(lists_v, lists_s, lc.at[1])
        to_scalar.start()
        for a in range(2):
            for side in range(2):
                wait(win_k.at[pl.ds(0, HALO)], fr.at[a, side])
        to_scalar.wait()

        def attend(start):
            spots = [[lists_s[start, t, e] for e in range(SEL)] for t in range(8)]

            def scores_of(t):
                keys = jnp.concatenate([win_k[w] for w in spots[t]], axis=0)
                query = win_q[start * 8 + t]
                return lax.dot_general(query, keys, (((1,), (1,)), ((), ())), preferred_element_type=jnp.float32)

            later = scores_of(0)
            for t in range(8):
                scores = later
                if t < 7:
                    later = scores_of(t + 1)
                peak = jnp.max(scores, axis=1, keepdims=True)
                weights = jnp.exp2((scores - peak) * EXP2)
                total = jnp.sum(weights, axis=1, keepdims=True)
                values = jnp.concatenate([win_v[w] for w in spots[t]], axis=0)
                mixed = jnp.dot(weights.astype(jnp.bfloat16), values, preferred_element_type=jnp.float32)
                win_o[start * 8 + t] = (mixed / total).astype(jnp.bfloat16)

        def quarter(i, carry):
            d = (i + 1) % 4
            start = (x + 4 - d) % 4
            wait(win_q.at[pl.ds(start * 8, 8)], yr.at[2, start])
            attend(start)

            def send(peer, carry):
                block = win_o.at[pl.ds(start * 8 + peer * 2, 2)]
                to = {"head": peer, "blk": z * 8 + core * 4 + x}
                local = own_row & (peer == head)

                @pl.when(i < 3)
                def _():
                    place = relay_o.at[start, :, :, pl.ds(pl.multiple_of(mine * HD, HD), HD)]
                    either(local, block, place, oys, oyr.at[d], to)

                @pl.when(i == 3)
                def _():
                    place = out_hbm.at[:, :, pl.ds(pl.multiple_of((3 * x + mine) * HD, HD), HD)]
                    either(local, block, place, oys, oxr, to)

                return carry

            lax.fori_loop(0, 4, send, 0)

            @pl.when(i >= 1)
            def _():
                out_x(i)

            return carry

        lax.fori_loop(0, 4, quarter, 0)

    @pl.when(jnp.logical_not(active))
    def _():
        for d in range(1, 4):
            out_x(d)

    wait(out_hbm, oxr)
    wait(relay_o.at[pl.ds(0, 3)], oxs)
    for d in range(3):
        wait(lists_r.at[x], ls)
    for a in (0, 2):
        wait(relay_k.at[pl.ds(0, 3)], xs.at[a])
    wait(relay_v.at[pl.ds(0, 3), pl.ds(0, 3)], xs.at[1])
    itself = own_row & active

    @pl.when(itself)
    def _():
        for a in (0, 2):
            wait(win_q.at[pl.ds(0, 16)], ys.at[a])
        wait(win_q.at[pl.ds(0, 24)], oys)

    @pl.when(jnp.logical_not(itself))
    def _():
        for a in (0, 2):
            wait(win_q.at[pl.ds(0, 24)], ys.at[a])

    @pl.when(active)
    def _():
        wait(win_q.at[pl.ds(0, 20)], ys.at[1])

    @pl.when(jnp.logical_not(active))
    def _():
        wait(win_q.at[pl.ds(0, 24)], ys.at[1])

    @pl.when(active & jnp.logical_not(own_row))
    def _():
        wait(win_q, oys)

    @pl.when(active)
    def _():
        for a in range(2):
            wait(win_q, fs.at[a])

    @pl.when(head == 0)
    def _():
        for j in range(2):
            wait(lists_v, ls)

        @pl.when(jnp.logical_not(itself))
        def _():
            wait(lists_v, ls)


def local(queries, key_rows, value_rows, tile_lists):
    bf16, dma = jnp.bfloat16, pltpu.SemaphoreType.DMA
    relay = pltpu.VMEM((4, 2, TILE, GROUP), bf16)
    spots = (tile_lists + (256 + HALO - ROW * (lax.axis_index("blk") // 4))) % 256
    tiles = (2, TILE, queries.shape[1])
    result = pl.pallas_call(
        kernel,
        out_shape=jax.ShapeDtypeStruct(tiles, bf16),
        in_specs=[pl.BlockSpec(memory_space=pl.ANY)] * 4,
        out_specs=pl.BlockSpec(memory_space=pl.ANY),
        scratch_shapes=[
            relay, pltpu.VMEM((4, 3, 2, TILE, HD), bf16), relay, relay,
            pltpu.VMEM((2 * ROW, TILE, HD), bf16), pltpu.VMEM((2 * ROW, TILE, HD), bf16),
            pltpu.VMEM((ROW, TILE, HD), bf16), pltpu.VMEM((ROW, TILE, HD), bf16),
            pltpu.VMEM((4, 8, SEL), jnp.int32), pltpu.VMEM((4, 8, SEL), jnp.int32), pltpu.SMEM((4, 8, SEL), jnp.int32),
            dma((3,)), dma((3, 4)), dma((3,)), dma((3, 4)), dma((2,)), dma((2, 2)),
            dma, dma((4,)), dma, dma((2,)), dma, dma((4,)), dma, dma,
        ],
        compiler_params=pltpu.CompilerParams(collective_id=0, has_side_effects=True, vmem_limit_bytes=56 * 2**20),
        cost_estimate=pl.CostEstimate(flops=4 * 10**9, bytes_accessed=8 * 10**6, transcendentals=8 * 10**6),
    )(queries.reshape(tiles), key_rows.reshape(tiles), value_rows.reshape(tiles), spots)
    return result.reshape(queries.shape)


def solution(mesh):
    tokens = P(("blk", "head"), None)
    return jax.shard_map(
        local, mesh=mesh, in_specs=(tokens, tokens, tokens, P("blk", None)), out_specs=tokens, check_vma=False
    )
```

```python
import functools

import jax
import jax.numpy as jnp
from jax import lax
from jax.experimental import pallas as pl
from jax.experimental.pallas import tpu as pltpu
from jax.sharding import PartitionSpec as P

MESH = pl.DeviceIdType.MESH
HD = 128
TILE = 128
SEL = 16
GROUP = 3 * HD
ROW = 32
EXP2 = HD ** -0.5 * 1.4426950408889634


def kernel(q_hbm, k_hbm, v_hbm, lists_hbm, out_hbm, relay_k, relay_v, relay_q, relay_p, relay_o, near_k, near_v, far_k, far_v, win_q,
           win_o, lists_r, lists_v, lists_w, lists_s, xs, xr, ys, yr, fs, fr, fl, ls, lxr, lyr, lc, oys, oyr, oxs, oxr):
    head, blk = lax.axis_index("head"), lax.axis_index("blk")
    x, y_lo, z = blk % 4, (blk // 4) % 2, blk // 8
    core = head % 2
    y = (head // 2) * 2 + y_lo
    mine = (y + 7 - x) % 4
    active = mine < 3
    own_row = core == y_lo

    def device(dx, dy, dz, dc):
        return {"head": (dy // 2) * 2 + dc, "blk": dz * 8 + (dy % 2) * 4 + dx}

    def remote(src, dst, send, recv, to):
        return pltpu.make_async_remote_copy(
            src_ref=src, dst_ref=dst, send_sem=send, recv_sem=recv, device_id=to, device_id_type=MESH
        )

    def wait(ref, sem):
        pltpu.make_async_copy(ref, ref, sem).wait()

    def either(local, src, dst, send, recv, to):
        @pl.when(local)
        def _():
            pltpu.make_async_copy(src, dst, recv).start()

        @pl.when(jnp.logical_not(local))
        def _():
            remote(src, dst, send, recv, to).start()

    barrier = pltpu.get_barrier_semaphore()
    for d in range(1, 4):
        for c in range(2):
            pl.semaphore_signal(barrier, inc=1, device_id=device((x + d) % 4, y, z, c), device_id_type=MESH)
            pl.semaphore_signal(barrier, inc=1, device_id=device(x, (y + d) % 4, z, c), device_id_type=MESH)
    pl.semaphore_signal(barrier, inc=1, device_id=device(x, y, z, 1 - core), device_id_type=MESH)
    across = device(x, y, (z + 2 * core + 3) % 4, 1 - core)
    pl.semaphore_signal(barrier, inc=1, device_id=across, device_id_type=MESH)
    pl.semaphore_wait(barrier, 14)

    arrays = (
        (k_hbm, relay_k, near_k, 0, 2),
        (v_hbm, relay_v, near_v, 0, 2),
        (q_hbm, relay_q, win_q, 0, 1),
        (q_hbm, relay_p, win_q, 1, 1),
    )

    def turn(i, row):
        return (2 * (1 - row) + 2 * (i // 2)) % 4 + (x + 1 + i) % 2

    def along_x(a):
        src, relay, _, tile, count = arrays[a]
        for d in (2, 1, 3):
            to = (x + d) % 4
            columns = pl.ds(pl.multiple_of(to * GROUP, GROUP), GROUP)
            block = src.at[pl.ds(tile, count), :, columns]
            remote(block, relay.at[x], xs.at[a], xr.at[a, d], device(to, y, z, core)).start()

    def then_along_y(a, start, first):
        src, relay, window, tile, count = arrays[a]
        base = tile if a >= 2 else 16 * y_lo
        if not first:
            wait(relay.at[start], xr.at[a, (x + 4 - start) % 4])

        def one(j, carry):
            to = (x + 1 + j) % 4
            if first:
                block = src.at[pl.ds(tile, count), :, pl.ds(pl.multiple_of((3 * x + j) * HD, HD), HD)]
            else:
                block = relay.at[start, :, :, pl.ds(pl.multiple_of(j * HD, HD), HD)]
            place = window.at[pl.ds(base + start * 8 + head * 2, count)]
            either(own_row & (to == y), block, place, ys.at[a], yr.at[min(a, 2), start], device(x, to, z, y_lo))
            return carry

        lax.fori_loop(0, 3, one, 0)

    def others_along_y(a, i):
        start = turn(i, y_lo)

        @pl.when(start != x)
        def _():
            then_along_y(a, start, False)

    def along_y(a):
        src, relay, _, tile, count = arrays[a]
        for d in (2, 1, 3):
            to = (y + d) % 4

            def one(k, carry):
                column = (to + 1 + k) % 4
                columns = pl.ds(pl.multiple_of((3 * column + 2 - k) * HD, HD), HD)
                block = src.at[pl.ds(tile, count), :, columns]
                remote(block, relay.at[y, k], xs.at[a], xr.at[a, d], device(x, to, z, core)).start()
                return carry

            lax.fori_loop(0, 3, one, 0)

    def then_along_x(a, d):
        src, relay, window, tile, count = arrays[a]
        source = (y + 4 - d) % 4
        base = tile if a >= 2 else 16 * (source % 2)
        if d:
            wait(relay.at[source, pl.ds(0, 3)], xr.at[a, d])

        def one(k, carry):
            to = (y + 1 + k) % 4
            if d:
                block = relay.at[source, k]
            else:
                block = src.at[pl.ds(tile, count), :, pl.ds(pl.multiple_of((3 * to + 2 - k) * HD, HD), HD)]
            peer = (source // 2) * 2 + core
            place = window.at[pl.ds(base + x * 8 + peer * 2, count)]
            local = (to == x) & (source % 2 == core)
            either(local, block, place, ys.at[a], yr.at[min(a, 2), x], device(to, y, z, source % 2))
            return carry

        lax.fori_loop(0, 3, one, 0)

    sibling = device(x, y, z, 1 - core)

    def forward(a, start):
        near, far = ((near_k, far_k), (near_v, far_v))[a]
        block = near.at[pl.ds(16 * core + start * 8, 8)]
        wait(block, yr.at[a, start])

        @pl.when(start // 2 == core)
        def _():
            place = far.at[pl.ds(32 * (1 - core) + (start % 2) * 8, 8)]
            remote(block, place, fs.at[a], fr.at[a, 1], across).start()

        @pl.when(start // 2 != core)
        def _():
            place = near.at[pl.ds(32 * core + (start % 2) * 8, 8)]
            remote(block, place, fs.at[a], fr.at[a, 0], sibling).start()

        pltpu.make_async_copy(block, far.at[pl.ds(16 * (1 - core) + start * 8, 8)], fl.at[a]).start()

    for d in range(1, 4):
        remote(lists_hbm, lists_r.at[x], ls, lxr.at[d], device((x + d) % 4, y, z, core)).start()
    own_lists = pltpu.make_async_copy(lists_hbm, lists_r.at[x], lc.at[0])
    own_lists.start()

    along_x(0)
    along_y(1)
    then_along_y(0, x, True)
    then_along_x(1, 0)
    for i, d in ((2, 2), (3, 1), (0, 3), (1, None)):
        others_along_y(0, i)
        if d:
            then_along_x(1, d)
    along_x(2)
    along_y(3)
    then_along_y(2, x, True)
    then_along_x(3, 0)

    own_lists.wait()
    for d in range(1, 4):
        wait(lists_r.at[x], lxr.at[d])

    @pl.when(head == 0)
    def _():
        for j in range(3):
            to = (x + 1 + j) % 4
            either(own_row & (to == y), lists_r, lists_v, ls, lyr, device(x, to, z, y_lo))

    @pl.when(active)
    def _():
        for i in (2, 3, 0, 1):
            for a in range(2):
                forward(a, turn(i, core))

    for i, d in ((0, 2), (1, 1), (2, 3), (3, None)):
        others_along_y(2, i)
        if d:
            then_along_x(3, d)

    def out_x(i):
        to = turn(i, y_lo)

        @pl.when(to != x)
        def _():
            wait(relay_o.at[to], oyr.at[(x + 4 - to) % 4])
            columns = pl.ds(pl.multiple_of(x * GROUP, GROUP), GROUP)
            remote(relay_o.at[to], out_hbm.at[:, :, columns], oxs, oxr, device(to, y, z, core)).start()

    @pl.when(active)
    def _():
        wait(lists_v, lyr)
        for i in range(4):
            place = (lists_v[i] + (272 - ROW * (2 * z + core) - 16 * (i // 2))) & 255
            lists_w[i] = jnp.minimum(place, ROW + 15)
        to_scalar = pltpu.make_async_copy(lists_w, lists_s, lc.at[1])
        to_scalar.start()
        for a in range(2):
            wait(near_k.at[pl.ds(0, 16)], fr.at[a, 0])
        to_scalar.wait()

        def attend(start, keys_ref, values_ref):
            spots = [[lists_s[start, t, e] for e in range(SEL)] for t in range(8)]

            def scores_of(t):
                keys = jnp.concatenate([keys_ref[w] for w in spots[t]], axis=0)
                query = win_q[start * 8 + t]
                return lax.dot_general(query, keys, (((1,), (1,)), ((), ())), preferred_element_type=jnp.float32)

            later = scores_of(0)
            for t in range(8):
                scores = later
                if t < 7:
                    later = scores_of(t + 1)
                peak = jnp.max(scores, axis=1, keepdims=True)
                weights = jnp.exp2((scores - peak) * EXP2)
                total = jnp.sum(weights, axis=1, keepdims=True)
                values = jnp.concatenate([values_ref[w] for w in spots[t]], axis=0)
                mixed = jnp.dot(weights.astype(jnp.bfloat16), values, preferred_element_type=jnp.float32)
                win_o[start * 8 + t] = (mixed / total).astype(jnp.bfloat16)

        def quarter(i, keys_ref, values_ref):
            start = turn(i, core)
            wait(win_q.at[pl.ds(start * 8, 8)], yr.at[2, start])
            attend(start, keys_ref, values_ref)

            def send(peer, carry):
                block = win_o.at[pl.ds(start * 8 + peer * 2, 2)]
                to = {"head": peer, "blk": z * 8 + core * 4 + x}
                local = own_row & (peer == head)

                @pl.when(start != x)
                def _():
                    place = relay_o.at[start, :, :, pl.ds(pl.multiple_of(mine * HD, HD), HD)]
                    either(local, block, place, oys, oyr.at[(x + 4 - start) % 4], to)

                @pl.when(start == x)
                def _():
                    place = out_hbm.at[:, :, pl.ds(pl.multiple_of((3 * x + mine) * HD, HD), HD)]
                    either(local, block, place, oys, oxr, to)

                return carry

            lax.fori_loop(0, 4, send, 0)

        def first_half(i, carry):
            quarter(i, near_k, near_v)

            @pl.when(i == 1)
            def _():
                out_x(0)

            return carry

        def second_half(i, carry):
            quarter(i, far_k, far_v)
            out_x(i - 1)
            return carry

        lax.fori_loop(0, 2, first_half, 0)
        for a in range(2):
            wait(far_k.at[pl.ds(0, 16)], fr.at[a, 1])
            wait(far_k.at[pl.ds(0, 32)], fl.at[a])
        lax.fori_loop(2, 4, second_half, 0)
        out_x(3)

    @pl.when(jnp.logical_not(active))
    def _():
        for i in range(4):
            out_x(i)

    wait(out_hbm, oxr)
    wait(relay_o.at[pl.ds(0, 3)], oxs)
    for d in range(3):
        wait(lists_r.at[x], ls)
    wait(relay_k.at[pl.ds(0, 3)], xs.at[0])
    wait(relay_v.at[pl.ds(0, 3), pl.ds(0, 3)], xs.at[1])
    wait(relay_q.at[pl.ds(0, 3)], xs.at[2])
    wait(relay_p.at[pl.ds(0, 3), pl.ds(0, 3)], xs.at[3])
    itself = own_row & active

    @pl.when(itself)
    def _():
        wait(win_q.at[pl.ds(0, 16)], ys.at[0])
        wait(win_q.at[pl.ds(0, 8)], ys.at[2])
        wait(win_q.at[pl.ds(0, 24)], oys)

    @pl.when(jnp.logical_not(itself))
    def _():
        wait(win_q.at[pl.ds(0, 24)], ys.at[0])
        wait(win_q.at[pl.ds(0, 12)], ys.at[2])

    @pl.when(active)
    def _():
        wait(win_q.at[pl.ds(0, 20)], ys.at[1])
        wait(win_q.at[pl.ds(0, 10)], ys.at[3])

    @pl.when(jnp.logical_not(active))
    def _():
        wait(win_q.at[pl.ds(0, 24)], ys.at[1])
        wait(win_q.at[pl.ds(0, 12)], ys.at[3])

    @pl.when(active & jnp.logical_not(own_row))
    def _():
        wait(win_q, oys)

    @pl.when(active)
    def _():
        for a in range(2):
            wait(win_q, fs.at[a])

    @pl.when(head == 0)
    def _():
        for j in range(2):
            wait(lists_v, ls)

        @pl.when(jnp.logical_not(itself))
        def _():
            wait(lists_v, ls)


def local(queries, key_rows, value_rows, tile_lists):
    bf16, dma = jnp.bfloat16, pltpu.SemaphoreType.DMA
    relay = pltpu.VMEM((4, 2, TILE, GROUP), bf16)
    window = pltpu.VMEM((ROW + 16, TILE, HD), bf16)
    lists = pltpu.VMEM((4, 8, SEL), jnp.int32)
    tiles = (2, TILE, queries.shape[1])
    result = pl.pallas_call(
        kernel,
        out_shape=jax.ShapeDtypeStruct(tiles, bf16),
        in_specs=[pl.BlockSpec(memory_space=pl.ANY)] * 4,
        out_specs=pl.BlockSpec(memory_space=pl.ANY),
        scratch_shapes=[
            relay, pltpu.VMEM((4, 3, 2, TILE, HD), bf16),
            pltpu.VMEM((4, 1, TILE, GROUP), bf16), pltpu.VMEM((4, 3, 1, TILE, HD), bf16), relay,
            window, window, window, window,
            pltpu.VMEM((ROW, TILE, HD), bf16), pltpu.VMEM((ROW, TILE, HD), bf16),
            lists, lists, lists, pltpu.SMEM((4, 8, SEL), jnp.int32),
            dma((4,)), dma((4, 4)), dma((4,)), dma((3, 4)), dma((2,)), dma((2, 2)), dma((2,)),
            dma, dma((4,)), dma, dma((2,)), dma, dma((4,)), dma, dma,
        ],
        compiler_params=pltpu.CompilerParams(collective_id=0, has_side_effects=True, vmem_limit_bytes=56 * 2**20),
        cost_estimate=pl.CostEstimate(flops=4 * 10**9, bytes_accessed=8 * 10**6, transcendentals=8 * 10**6),
    )(queries.reshape(tiles), key_rows.reshape(tiles), value_rows.reshape(tiles), tile_lists)
    return result.reshape(queries.shape)


def solution(mesh):
    tokens = P(("blk", "head"), None)
    return jax.shard_map(
        local, mesh=mesh, in_specs=(tokens, tokens, tokens, P("blk", None)), out_specs=tokens, check_vma=False
    )
```

```python
import functools

import jax
import jax.numpy as jnp
from jax import lax
from jax.experimental import pallas as pl
from jax.experimental.pallas import tpu as pltpu
from jax.sharding import PartitionSpec as P

MESH = pl.DeviceIdType.MESH
HD = 128
TILE = 128
SEL = 16
GROUP = 3 * HD
ROW = 32
EXP2 = HD ** -0.5 * 1.4426950408889634


def kernel(q_hbm, k_hbm, v_hbm, lists_hbm, out_hbm, relay_k, relay_v, relay_q, relay_p, relay_o, relay_r, near_k, near_v, far_k, far_v, win_q,
           win_o, lists_r, lists_v, lists_w, lists_s, xs, xr, ys, yr, fs, fr, fl, ls, lxr, lyr, lc, oys, oyr, oxs, oxr, ofs, ofr, ors):
    head, blk = lax.axis_index("head"), lax.axis_index("blk")
    x, y_lo, z = blk % 4, (blk // 4) % 2, blk // 8
    core = head % 2
    y = (head // 2) * 2 + y_lo
    mine = (y + 7 - x) % 4
    active = mine < 3
    own_row = core == y_lo

    def device(dx, dy, dz, dc):
        return {"head": (dy // 2) * 2 + dc, "blk": dz * 8 + (dy % 2) * 4 + dx}

    def remote(src, dst, send, recv, to):
        return pltpu.make_async_remote_copy(
            src_ref=src, dst_ref=dst, send_sem=send, recv_sem=recv, device_id=to, device_id_type=MESH
        )

    def wait(ref, sem):
        pltpu.make_async_copy(ref, ref, sem).wait()

    def either(local, src, dst, send, recv, to):
        @pl.when(local)
        def _():
            pltpu.make_async_copy(src, dst, recv).start()

        @pl.when(jnp.logical_not(local))
        def _():
            remote(src, dst, send, recv, to).start()

    barrier = pltpu.get_barrier_semaphore()
    for d in range(1, 4):
        for c in range(2):
            pl.semaphore_signal(barrier, inc=1, device_id=device((x + d) % 4, y, z, c), device_id_type=MESH)
            pl.semaphore_signal(barrier, inc=1, device_id=device(x, (y + d) % 4, z, c), device_id_type=MESH)
    pl.semaphore_signal(barrier, inc=1, device_id=device(x, y, z, 1 - core), device_id_type=MESH)
    across = device(x, y, (z + 2 * core + 3) % 4, 1 - core)
    pl.semaphore_signal(barrier, inc=1, device_id=across, device_id_type=MESH)
    pl.semaphore_wait(barrier, 14)

    arrays = (
        (k_hbm, relay_k, near_k, 0, 2),
        (v_hbm, relay_v, near_v, 0, 2),
        (q_hbm, relay_q, win_q, 0, 1),
        (q_hbm, relay_p, win_q, 1, 1),
    )

    def turn(i, row):
        return (2 * (1 - row) + 2 * (i // 2)) % 4 + (x + 1 + i) % 2

    def along_x(a):
        src, relay, _, tile, count = arrays[a]
        for d in (2, 1, 3):
            to = (x + d) % 4
            columns = pl.ds(pl.multiple_of(to * GROUP, GROUP), GROUP)
            block = src.at[pl.ds(tile, count), :, columns]
            remote(block, relay.at[x], xs.at[a], xr.at[a, d], device(to, y, z, core)).start()

    def then_along_y(a, start, first):
        src, relay, window, tile, count = arrays[a]
        base = tile if a >= 2 else 16 * y_lo
        if not first:
            wait(relay.at[start], xr.at[a, (x + 4 - start) % 4])

        def one(j, carry):
            to = (x + 1 + j) % 4
            if first:
                block = src.at[pl.ds(tile, count), :, pl.ds(pl.multiple_of((3 * x + j) * HD, HD), HD)]
            else:
                block = relay.at[start, :, :, pl.ds(pl.multiple_of(j * HD, HD), HD)]
            place = window.at[pl.ds(base + start * 8 + head * 2, count)]
            either(own_row & (to == y), block, place, ys.at[a], yr.at[min(a, 2), start], device(x, to, z, y_lo))
            return carry

        lax.fori_loop(0, 3, one, 0)

    def others_along_y(a, i):
        start = turn(i, y_lo)

        @pl.when(start != x)
        def _():
            then_along_y(a, start, False)

    def along_y(a):
        src, relay, _, tile, count = arrays[a]
        for d in (2, 1, 3):
            to = (y + d) % 4

            def one(k, carry):
                column = (to + 1 + k) % 4
                columns = pl.ds(pl.multiple_of((3 * column + 2 - k) * HD, HD), HD)
                block = src.at[pl.ds(tile, count), :, columns]
                remote(block, relay.at[y, k], xs.at[a], xr.at[a, d], device(x, to, z, core)).start()
                return carry

            lax.fori_loop(0, 3, one, 0)

    def then_along_x(a, d):
        src, relay, window, tile, count = arrays[a]
        source = (y + 4 - d) % 4
        base = tile if a >= 2 else 16 * (source % 2)
        if d:
            wait(relay.at[source, pl.ds(0, 3)], xr.at[a, d])

        def one(k, carry):
            to = (y + 1 + k) % 4
            if d:
                block = relay.at[source, k]
            else:
                block = src.at[pl.ds(tile, count), :, pl.ds(pl.multiple_of((3 * to + 2 - k) * HD, HD), HD)]
            peer = (source // 2) * 2 + core
            place = window.at[pl.ds(base + x * 8 + peer * 2, count)]
            local = (to == x) & (source % 2 == core)
            either(local, block, place, ys.at[a], yr.at[min(a, 2), x], device(to, y, z, source % 2))
            return carry

        lax.fori_loop(0, 3, one, 0)

    sibling = device(x, y, z, 1 - core)

    def forward(a, start):
        near, far = ((near_k, far_k), (near_v, far_v))[a]
        block = near.at[pl.ds(16 * core + start * 8, 8)]
        wait(block, yr.at[a, start])

        @pl.when(start // 2 == core)
        def _():
            place = far.at[pl.ds(32 * (1 - core) + (start % 2) * 8, 8)]
            remote(block, place, fs.at[a], fr.at[a, 1], across).start()

        @pl.when(start // 2 != core)
        def _():
            place = near.at[pl.ds(32 * core + (start % 2) * 8, 8)]
            remote(block, place, fs.at[a], fr.at[a, 0], sibling).start()

        pltpu.make_async_copy(block, far.at[pl.ds(16 * (1 - core) + start * 8, 8)], fl.at[a]).start()

    for d in range(1, 4):
        remote(lists_hbm, lists_r.at[x], ls, lxr.at[d], device((x + d) % 4, y, z, core)).start()
    own_lists = pltpu.make_async_copy(lists_hbm, lists_r.at[x], lc.at[0])
    own_lists.start()

    along_x(0)
    along_y(1)
    then_along_y(0, x, True)
    then_along_x(1, 0)
    for i, d in ((2, 2), (3, 1), (0, 3), (1, None)):
        others_along_y(0, i)
        if d:
            then_along_x(1, d)
    along_x(2)
    along_y(3)
    then_along_y(2, x, True)
    then_along_x(3, 0)

    own_lists.wait()
    for d in range(1, 4):
        wait(lists_r.at[x], lxr.at[d])

    @pl.when(head == 0)
    def _():
        for j in range(3):
            to = (x + 1 + j) % 4
            either(own_row & (to == y), lists_r, lists_v, ls, lyr, device(x, to, z, y_lo))

    @pl.when(active)
    def _():
        for i in (2, 3, 0, 1):
            for a in range(2):
                forward(a, turn(i, core))

    for i, d in ((0, 2), (1, 1), (2, 3), (3, None)):
        others_along_y(2, i)
        if d:
            then_along_x(3, d)

    def out_x(i):
        to = turn(i, y_lo)

        @pl.when(to != x)
        def _():
            wait(relay_o.at[to], oyr.at[(x + 4 - to) % 4])
            columns = pl.ds(pl.multiple_of(x * GROUP, GROUP), GROUP)
            remote(relay_o.at[to], out_hbm.at[pl.ds(0, 1), :, columns], oxs, oxr, device(to, y, z, core)).start()

    def out_y(i):
        for k in range(1, 4):
            start = (x + k) % 4
            theirs = 2 * (1 - (x // 2 + core) % 2) + (x + start + 1) % 2

            @pl.when((start != y) & (theirs == i))
            def _():
                wait(relay_r.at[start], ofr.at[start])
                column = 3 * start + (y + 7 - start) % 4

                def one(peer, carry):
                    block = relay_r.at[start, pl.ds(peer, 1)]
                    place = out_hbm.at[pl.ds(1, 1), :, pl.ds(pl.multiple_of(column * HD, HD), HD)]
                    to = {"head": peer, "blk": z * 8 + core * 4 + x}
                    either(own_row & (peer == head), block, place, ors, oxr, to)
                    return carry

                lax.fori_loop(0, 4, one, 0)

    @pl.when(active)
    def _():
        wait(lists_v, lyr)
        for i in range(4):
            place = (lists_v[i] + (272 - ROW * (2 * z + core) - 16 * (i // 2))) & 255
            lists_w[i] = jnp.minimum(place, ROW + 15)
        to_scalar = pltpu.make_async_copy(lists_w, lists_s, lc.at[1])
        to_scalar.start()
        for a in range(2):
            wait(near_k.at[pl.ds(0, 16)], fr.at[a, 0])
        to_scalar.wait()

        def attend(start, keys_ref, values_ref):
            spots = [[lists_s[start, t, e] for e in range(SEL)] for t in range(8)]

            def scores_of(t):
                keys = jnp.concatenate([keys_ref[w] for w in spots[t]], axis=0)
                query = win_q[start * 8 + t]
                return lax.dot_general(query, keys, (((1,), (1,)), ((), ())), preferred_element_type=jnp.float32)

            later = scores_of(0)
            for t in range(8):
                scores = later
                if t < 7:
                    later = scores_of(t + 1)
                peak = jnp.max(scores, axis=1, keepdims=True)
                weights = jnp.exp2((scores - peak) * EXP2)
                total = jnp.sum(weights, axis=1, keepdims=True)
                values = jnp.concatenate([values_ref[w] for w in spots[t]], axis=0)
                mixed = jnp.dot(weights.astype(jnp.bfloat16), values, preferred_element_type=jnp.float32)
                win_o[t % 2, start * 4 + t // 2] = (mixed / total).astype(jnp.bfloat16)

        def quarter(i, keys_ref, values_ref):
            start = turn(i, core)
            wait(win_q.at[pl.ds(start * 8, 8)], yr.at[2, start])
            attend(start, keys_ref, values_ref)

            @pl.when(start != x)
            def _():
                block = win_o.at[1, pl.ds(start * 4, 4)]
                remote(block, relay_r.at[x], ofs, ofr.at[x], device(start, y, z, core)).start()

            def send(peer, carry):
                to = {"head": peer, "blk": z * 8 + core * 4 + x}
                local = own_row & (peer == head)

                @pl.when(start != x)
                def _():
                    block = win_o.at[0, pl.ds(start * 4 + peer, 1)]
                    place = relay_o.at[start, :, :, pl.ds(pl.multiple_of(mine * HD, HD), HD)]
                    either(local, block, place, oys, oyr.at[(x + 4 - start) % 4], to)

                @pl.when(start == x)
                def _():
                    block = win_o.at[:, start * 4 + peer]
                    place = out_hbm.at[:, :, pl.ds(pl.multiple_of((3 * x + mine) * HD, HD), HD)]
                    either(local, block, place, oys, oxr, to)

                return carry

            lax.fori_loop(0, 4, send, 0)

        def first_half(i, carry):
            quarter(i, near_k, near_v)

            @pl.when(i == 1)
            def _():
                out_x(0)
                out_y(0)

            return carry

        def second_half(i, carry):
            quarter(i, far_k, far_v)
            out_x(i - 1)
            out_y(i - 1)
            return carry

        lax.fori_loop(0, 2, first_half, 0)
        for a in range(2):
            wait(far_k.at[pl.ds(0, 16)], fr.at[a, 1])
            wait(far_k.at[pl.ds(0, 32)], fl.at[a])
        lax.fori_loop(2, 4, second_half, 0)
        out_x(3)
        out_y(3)

    @pl.when(jnp.logical_not(active))
    def _():
        for i in range(4):
            out_x(i)
            out_y(i)

    wait(out_hbm, oxr)
    wait(relay_o.at[pl.ds(0, 3)], oxs)
    for d in range(3):
        wait(lists_r.at[x], ls)
    wait(relay_k.at[pl.ds(0, 3)], xs.at[0])
    wait(relay_v.at[pl.ds(0, 3), pl.ds(0, 3)], xs.at[1])
    wait(relay_q.at[pl.ds(0, 3)], xs.at[2])
    wait(relay_p.at[pl.ds(0, 3), pl.ds(0, 3)], xs.at[3])
    itself = own_row & active

    @pl.when(itself)
    def _():
        wait(win_q.at[pl.ds(0, 16)], ys.at[0])
        wait(win_q.at[pl.ds(0, 8)], ys.at[2])
        wait(win_q.at[pl.ds(0, 15)], oys)

    @pl.when(jnp.logical_not(itself))
    def _():
        wait(win_q.at[pl.ds(0, 24)], ys.at[0])
        wait(win_q.at[pl.ds(0, 12)], ys.at[2])

    @pl.when(active)
    def _():
        wait(win_q.at[pl.ds(0, 20)], ys.at[1])
        wait(win_q.at[pl.ds(0, 10)], ys.at[3])

    @pl.when(jnp.logical_not(active))
    def _():
        wait(win_q.at[pl.ds(0, 24)], ys.at[1])
        wait(win_q.at[pl.ds(0, 12)], ys.at[3])

    for idle, own, count in ((0, 0, 8), (0, 1, 6), (1, 0, 12), (1, 1, 9)):

        @pl.when((active if not idle else jnp.logical_not(active)) & (own_row if own else jnp.logical_not(own_row)))
        def _():
            wait(win_q.at[pl.ds(0, count)], ors)

    @pl.when(active & jnp.logical_not(own_row))
    def _():
        wait(win_q.at[pl.ds(0, 20)], oys)

    @pl.when(active)
    def _():
        wait(win_q.at[pl.ds(0, 12)], ofs)
        for a in range(2):
            wait(win_q, fs.at[a])

    @pl.when(head == 0)
    def _():
        for j in range(2):
            wait(lists_v, ls)

        @pl.when(jnp.logical_not(itself))
        def _():
            wait(lists_v, ls)


def local(queries, key_rows, value_rows, tile_lists):
    bf16, dma = jnp.bfloat16, pltpu.SemaphoreType.DMA
    relay = pltpu.VMEM((4, 2, TILE, GROUP), bf16)
    window = pltpu.VMEM((ROW + 16, TILE, HD), bf16)
    lists = pltpu.VMEM((4, 8, SEL), jnp.int32)
    tiles = (2, TILE, queries.shape[1])
    result = pl.pallas_call(
        kernel,
        out_shape=jax.ShapeDtypeStruct(tiles, bf16),
        in_specs=[pl.BlockSpec(memory_space=pl.ANY)] * 4,
        out_specs=pl.BlockSpec(memory_space=pl.ANY),
        scratch_shapes=[
            relay, pltpu.VMEM((4, 3, 2, TILE, HD), bf16),
            pltpu.VMEM((4, 1, TILE, GROUP), bf16), pltpu.VMEM((4, 3, 1, TILE, HD), bf16),
            pltpu.VMEM((4, 1, TILE, GROUP), bf16), pltpu.VMEM((4, 4, TILE, HD), bf16),
            window, window, window, window,
            pltpu.VMEM((ROW, TILE, HD), bf16), pltpu.VMEM((2, ROW // 2, TILE, HD), bf16),
            lists, lists, lists, pltpu.SMEM((4, 8, SEL), jnp.int32),
            dma((4,)), dma((4, 4)), dma((4,)), dma((3, 4)), dma((2,)), dma((2, 2)), dma((2,)),
            dma, dma((4,)), dma, dma((2,)), dma, dma((4,)), dma, dma, dma, dma((4,)), dma,
        ],
        compiler_params=pltpu.CompilerParams(collective_id=0, has_side_effects=True, vmem_limit_bytes=56 * 2**20),
        cost_estimate=pl.CostEstimate(flops=4 * 10**9, bytes_accessed=8 * 10**6, transcendentals=8 * 10**6),
    )(queries.reshape(tiles), key_rows.reshape(tiles), value_rows.reshape(tiles), tile_lists)
    return result.reshape(queries.shape)


def solution(mesh):
    tokens = P(("blk", "head"), None)
    return jax.shard_map(
        local, mesh=mesh, in_specs=(tokens, tokens, tokens, P("blk", None)), out_specs=tokens, check_vma=False
    )
```

```python
import functools

import jax
import jax.numpy as jnp
from jax import lax
from jax.experimental import pallas as pl
from jax.experimental.pallas import tpu as pltpu
from jax.sharding import PartitionSpec as P

MESH = pl.DeviceIdType.MESH
HD = 128
TILE = 128
SEL = 16
GROUP = 3 * HD
ROW = 32
EXP2 = HD ** -0.5 * 1.4426950408889634


def kernel(q_hbm, k_hbm, v_hbm, lists_hbm, out_hbm, relay_k, relay_v, relay_q, relay_p, relay_o, relay_r, near_k, near_v, far_k, far_v, win_q,
           win_o, lists_r, lists_v, lists_w, lists_s, xs, xr, ys, yr, fs, fr, fl, ls, lxr, lyr, lc, oys, oyr, oxs, oxr, ofs, ofr, ors):
    head, blk = lax.axis_index("head"), lax.axis_index("blk")
    x, y_lo, z = blk % 4, (blk // 4) % 2, blk // 8
    core = head % 2
    y = (head // 2) * 2 + y_lo
    mine = (y + 7 - x) % 4
    active = mine < 3
    own_row = core == y_lo

    def device(dx, dy, dz, dc):
        return {"head": (dy // 2) * 2 + dc, "blk": dz * 8 + (dy % 2) * 4 + dx}

    def remote(src, dst, send, recv, to):
        return pltpu.make_async_remote_copy(
            src_ref=src, dst_ref=dst, send_sem=send, recv_sem=recv, device_id=to, device_id_type=MESH
        )

    def wait(ref, sem):
        pltpu.make_async_copy(ref, ref, sem).wait()

    def either(local, src, dst, send, recv, to):
        @pl.when(local)
        def _():
            pltpu.make_async_copy(src, dst, recv).start()

        @pl.when(jnp.logical_not(local))
        def _():
            remote(src, dst, send, recv, to).start()

    barrier = pltpu.get_barrier_semaphore()
    for d in range(1, 4):
        for c in range(2):
            pl.semaphore_signal(barrier, inc=1, device_id=device((x + d) % 4, y, z, c), device_id_type=MESH)
            pl.semaphore_signal(barrier, inc=1, device_id=device(x, (y + d) % 4, z, c), device_id_type=MESH)
    pl.semaphore_signal(barrier, inc=1, device_id=device(x, y, z, 1 - core), device_id_type=MESH)
    across = device(x, y, (z + 2 * core + 3) % 4, 1 - core)
    pl.semaphore_signal(barrier, inc=1, device_id=across, device_id_type=MESH)
    pl.semaphore_wait(barrier, 14)

    arrays = (
        (k_hbm, relay_k, near_k, 0, 2),
        (v_hbm, relay_v, near_v, 0, 2),
        (q_hbm, relay_q, win_q, 0, 1),
        (q_hbm, relay_p, win_q, 1, 1),
    )

    def turn(i, row):
        late = (x // 2 + row) % 2
        return jnp.where(
            i == 3, x, jnp.where(i == 2 * (1 - late), x + 1 - 2 * (x % 2), 2 * (1 - x // 2) + (x + 3 + i - late) % 2)
        )

    def along_x(a):
        src, relay, _, tile, count = arrays[a]
        for d in (2, 1, 3):
            to = (x + d) % 4
            columns = pl.ds(pl.multiple_of(to * GROUP, GROUP), GROUP)
            block = src.at[pl.ds(tile, count), :, columns]
            remote(block, relay.at[x], xs.at[a], xr.at[a, d], device(to, y, z, core)).start()

    def then_along_y(a, start, first):
        src, relay, window, tile, count = arrays[a]
        base = tile if a >= 2 else 16 * y_lo
        if not first:
            wait(relay.at[start], xr.at[a, (x + 4 - start) % 4])

        def one(j, carry):
            to = (x + 1 + j) % 4
            if first:
                block = src.at[pl.ds(tile, count), :, pl.ds(pl.multiple_of((3 * x + j) * HD, HD), HD)]
            else:
                block = relay.at[start, :, :, pl.ds(pl.multiple_of(j * HD, HD), HD)]
            place = window.at[pl.ds(base + start * 8 + head * 2, count)]
            either(own_row & (to == y), block, place, ys.at[a], yr.at[min(a, 2), start], device(x, to, z, y_lo))
            return carry

        lax.fori_loop(0, 3, one, 0)

    def others_along_y(a, i):
        start = turn(i, y_lo)

        @pl.when(start != x)
        def _():
            then_along_y(a, start, False)

    def along_y(a):
        src, relay, _, tile, count = arrays[a]
        for d in (2, 1, 3):
            to = (y + d) % 4

            def one(k, carry):
                column = (to + 1 + k) % 4
                columns = pl.ds(pl.multiple_of((3 * column + 2 - k) * HD, HD), HD)
                block = src.at[pl.ds(tile, count), :, columns]
                remote(block, relay.at[y, k], xs.at[a], xr.at[a, d], device(x, to, z, core)).start()
                return carry

            lax.fori_loop(0, 3, one, 0)

    def then_along_x(a, d):
        src, relay, window, tile, count = arrays[a]
        source = (y + 4 - d) % 4
        base = tile if a >= 2 else 16 * (source % 2)
        if d:
            wait(relay.at[source, pl.ds(0, 3)], xr.at[a, d])

        def one(k, carry):
            to = (y + 1 + k) % 4
            if d:
                block = relay.at[source, k]
            else:
                block = src.at[pl.ds(tile, count), :, pl.ds(pl.multiple_of((3 * to + 2 - k) * HD, HD), HD)]
            peer = (source // 2) * 2 + core
            place = window.at[pl.ds(base + x * 8 + peer * 2, count)]
            local = (to == x) & (source % 2 == core)
            either(local, block, place, ys.at[a], yr.at[min(a, 2), x], device(to, y, z, source % 2))
            return carry

        lax.fori_loop(0, 3, one, 0)

    sibling = device(x, y, z, 1 - core)

    def forward(a, start):
        near, far = ((near_k, far_k), (near_v, far_v))[a]
        block = near.at[pl.ds(16 * core + start * 8, 8)]
        wait(block, yr.at[a, start])

        @pl.when(start // 2 == core)
        def _():
            place = far.at[pl.ds(32 * (1 - core) + (start % 2) * 8, 8)]
            remote(block, place, fs.at[a], fr.at[a, 1], across).start()

        @pl.when(start // 2 != core)
        def _():
            place = near.at[pl.ds(32 * core + (start % 2) * 8, 8)]
            remote(block, place, fs.at[a], fr.at[a, 0], sibling).start()

        pltpu.make_async_copy(block, far.at[pl.ds(16 * (1 - core) + start * 8, 8)], fl.at[a]).start()

    for d in range(1, 4):
        remote(lists_hbm, lists_r.at[x], ls, lxr.at[d], device((x + d) % 4, y, z, core)).start()
    own_lists = pltpu.make_async_copy(lists_hbm, lists_r.at[x], lc.at[0])
    own_lists.start()

    along_x(0)
    along_y(1)
    then_along_y(0, x, True)
    then_along_x(1, 0)
    for i, d in ((2, 2), (1, 1), (0, 3)):
        others_along_y(0, i)
        then_along_x(1, d)
    along_x(2)
    along_y(3)
    then_along_y(2, x, True)
    then_along_x(3, 0)

    own_lists.wait()
    for d in range(1, 4):
        wait(lists_r.at[x], lxr.at[d])

    @pl.when(head == 0)
    def _():
        for j in range(3):
            to = (x + 1 + j) % 4
            either(own_row & (to == y), lists_r, lists_v, ls, lyr, device(x, to, z, y_lo))

    @pl.when(active)
    def _():
        for i in (2, 1, 3, 0):
            for a in range(2):
                forward(a, turn(i, core))

    for i, d in ((0, 2), (1, 1), (2, 3)):
        others_along_y(2, i)
        then_along_x(3, d)

    def out_x(i):
        to = turn(i, y_lo)

        @pl.when(to != x)
        def _():
            wait(relay_o.at[to], oyr.at[(x + 4 - to) % 4])
            columns = pl.ds(pl.multiple_of(x * GROUP, GROUP), GROUP)
            remote(relay_o.at[to], out_hbm.at[pl.ds(0, 1), :, columns], oxs, oxr, device(to, y, z, core)).start()

    def out_y(i):
        for k in range(1, 4):
            start = (x + k) % 4
            late = (start // 2 + core) % 2
            theirs = jnp.where(x // 2 == start // 2, 2 * (1 - late), (x + start + 1) % 2 + late)

            @pl.when((start != y) & (theirs == i))
            def _():
                wait(relay_r.at[start], ofr.at[start])
                column = 3 * start + (y + 7 - start) % 4

                def one(peer, carry):
                    block = relay_r.at[start, pl.ds(peer, 1)]
                    place = out_hbm.at[pl.ds(1, 1), :, pl.ds(pl.multiple_of(column * HD, HD), HD)]
                    to = {"head": peer, "blk": z * 8 + core * 4 + x}
                    either(own_row & (peer == head), block, place, ors, oxr, to)
                    return carry

                lax.fori_loop(0, 4, one, 0)

    @pl.when(active)
    def _():
        wait(lists_v, lyr)
        for i in range(4):
            place = (lists_v[i] + (272 - ROW * (2 * z + core) - 16 * (i // 2))) & 255
            lists_w[i] = jnp.minimum(place, ROW + 15)
        to_scalar = pltpu.make_async_copy(lists_w, lists_s, lc.at[1])
        to_scalar.start()
        for a in range(2):
            wait(near_k.at[pl.ds(0, 16)], fr.at[a, 0])
        to_scalar.wait()

        def attend(start, keys_ref, values_ref):
            spots = [[lists_s[start, t, e] for e in range(SEL)] for t in range(8)]

            def scores_of(t):
                keys = jnp.concatenate([keys_ref[w] for w in spots[t]], axis=0)
                query = win_q[start * 8 + t]
                return lax.dot_general(query, keys, (((1,), (1,)), ((), ())), preferred_element_type=jnp.float32)

            later = scores_of(0)
            for t in range(8):
                scores = later
                if t < 7:
                    later = scores_of(t + 1)
                peak = jnp.max(scores, axis=1, keepdims=True)
                weights = jnp.exp2((scores - peak) * EXP2)
                total = jnp.sum(weights, axis=1, keepdims=True)
                values = jnp.concatenate([values_ref[w] for w in spots[t]], axis=0)
                mixed = jnp.dot(weights.astype(jnp.bfloat16), values, preferred_element_type=jnp.float32)
                win_o[t % 2, start * 4 + t // 2] = (mixed / total).astype(jnp.bfloat16)

        def quarter(i, carry):
            start = turn(i, core)
            wait(win_q.at[pl.ds(start * 8, 8)], yr.at[2, start])

            @pl.when(start // 2 != core)
            def _():
                attend(start, near_k, near_v)

            @pl.when((start // 2 == core) & (i == 2 - (x // 2 + core) % 2))
            def _():
                for a in range(2):
                    wait(far_k.at[pl.ds(0, 16)], fr.at[a, 1])
                    wait(far_k.at[pl.ds(0, 32)], fl.at[a])

            @pl.when(start // 2 == core)
            def _():
                attend(start, far_k, far_v)

            @pl.when(start != x)
            def _():
                block = win_o.at[1, pl.ds(start * 4, 4)]
                remote(block, relay_r.at[x], ofs, ofr.at[x], device(start, y, z, core)).start()

            def send(peer, carry):
                to = {"head": peer, "blk": z * 8 + core * 4 + x}
                local = own_row & (peer == head)

                @pl.when(start != x)
                def _():
                    block = win_o.at[0, pl.ds(start * 4 + peer, 1)]
                    place = relay_o.at[start, :, :, pl.ds(pl.multiple_of(mine * HD, HD), HD)]
                    either(local, block, place, oys, oyr.at[(x + 4 - start) % 4], to)

                @pl.when(start == x)
                def _():
                    block = win_o.at[:, start * 4 + peer]
                    place = out_hbm.at[:, :, pl.ds(pl.multiple_of((3 * x + mine) * HD, HD), HD)]
                    either(local, block, place, oys, oxr, to)

                return carry

            lax.fori_loop(0, 4, send, 0)
            return carry

        lax.fori_loop(0, 4, quarter, 0)
        for i in range(4):
            out_x(i)
            out_y(i)

    @pl.when(jnp.logical_not(active))
    def _():
        for i in range(4):
            out_x(i)
            out_y(i)

    wait(out_hbm, oxr)
    wait(relay_o.at[pl.ds(0, 3)], oxs)
    for d in range(3):
        wait(lists_r.at[x], ls)
    wait(relay_k.at[pl.ds(0, 3)], xs.at[0])
    wait(relay_v.at[pl.ds(0, 3), pl.ds(0, 3)], xs.at[1])
    wait(relay_q.at[pl.ds(0, 3)], xs.at[2])
    wait(relay_p.at[pl.ds(0, 3), pl.ds(0, 3)], xs.at[3])
    itself = own_row & active

    @pl.when(itself)
    def _():
        wait(win_q.at[pl.ds(0, 16)], ys.at[0])
        wait(win_q.at[pl.ds(0, 8)], ys.at[2])
        wait(win_q.at[pl.ds(0, 15)], oys)

    @pl.when(jnp.logical_not(itself))
    def _():
        wait(win_q.at[pl.ds(0, 24)], ys.at[0])
        wait(win_q.at[pl.ds(0, 12)], ys.at[2])

    @pl.when(active)
    def _():
        wait(win_q.at[pl.ds(0, 20)], ys.at[1])
        wait(win_q.at[pl.ds(0, 10)], ys.at[3])

    @pl.when(jnp.logical_not(active))
    def _():
        wait(win_q.at[pl.ds(0, 24)], ys.at[1])
        wait(win_q.at[pl.ds(0, 12)], ys.at[3])

    for idle, own, count in ((0, 0, 8), (0, 1, 6), (1, 0, 12), (1, 1, 9)):

        @pl.when((active if not idle else jnp.logical_not(active)) & (own_row if own else jnp.logical_not(own_row)))
        def _():
            wait(win_q.at[pl.ds(0, count)], ors)

    @pl.when(active & jnp.logical_not(own_row))
    def _():
        wait(win_q.at[pl.ds(0, 20)], oys)

    @pl.when(active)
    def _():
        wait(win_q.at[pl.ds(0, 12)], ofs)
        for a in range(2):
            wait(win_q, fs.at[a])

    @pl.when(head == 0)
    def _():
        for j in range(2):
            wait(lists_v, ls)

        @pl.when(jnp.logical_not(itself))
        def _():
            wait(lists_v, ls)


def local(queries, key_rows, value_rows, tile_lists):
    bf16, dma = jnp.bfloat16, pltpu.SemaphoreType.DMA
    relay = pltpu.VMEM((4, 2, TILE, GROUP), bf16)
    window = pltpu.VMEM((ROW + 16, TILE, HD), bf16)
    lists = pltpu.VMEM((4, 8, SEL), jnp.int32)
    tiles = (2, TILE, queries.shape[1])
    result = pl.pallas_call(
        kernel,
        out_shape=jax.ShapeDtypeStruct(tiles, bf16),
        in_specs=[pl.BlockSpec(memory_space=pl.ANY)] * 4,
        out_specs=pl.BlockSpec(memory_space=pl.ANY),
        scratch_shapes=[
            relay, pltpu.VMEM((4, 3, 2, TILE, HD), bf16),
            pltpu.VMEM((4, 1, TILE, GROUP), bf16), pltpu.VMEM((4, 3, 1, TILE, HD), bf16),
            pltpu.VMEM((4, 1, TILE, GROUP), bf16), pltpu.VMEM((4, 4, TILE, HD), bf16),
            window, window, window, window,
            pltpu.VMEM((ROW, TILE, HD), bf16), pltpu.VMEM((2, ROW // 2, TILE, HD), bf16),
            lists, lists, lists, pltpu.SMEM((4, 8, SEL), jnp.int32),
            dma((4,)), dma((4, 4)), dma((4,)), dma((3, 4)), dma((2,)), dma((2, 2)), dma((2,)),
            dma, dma((4,)), dma, dma((2,)), dma, dma((4,)), dma, dma, dma, dma((4,)), dma,
        ],
        compiler_params=pltpu.CompilerParams(collective_id=0, has_side_effects=True, vmem_limit_bytes=56 * 2**20),
        cost_estimate=pl.CostEstimate(flops=4 * 10**9, bytes_accessed=8 * 10**6, transcendentals=8 * 10**6),
    )(queries.reshape(tiles), key_rows.reshape(tiles), value_rows.reshape(tiles), tile_lists)
    return result.reshape(queries.shape)


def solution(mesh):
    tokens = P(("blk", "head"), None)
    return jax.shard_map(
        local, mesh=mesh, in_specs=(tokens, tokens, tokens, P("blk", None)), out_specs=tokens, check_vma=False
    )
```

```python
import functools

import jax
import jax.numpy as jnp
from jax import lax
from jax.experimental import pallas as pl
from jax.experimental.pallas import tpu as pltpu
from jax.sharding import PartitionSpec as P

MESH = pl.DeviceIdType.MESH
HD = 128
TILE = 128
SEL = 16
GROUP = 3 * HD
ROW = 32
EXP2 = HD ** -0.5 * 1.4426950408889634


def kernel(q_hbm, k_hbm, v_hbm, lists_hbm, out_hbm, relay_k, relay_v, relay_q, relay_p, relay_o, relay_r, near_k, near_v, far_k, far_v, win_q,
           win_o, lists_r, lists_v, lists_w, lists_s, xs, xr, ys, yr, fs, fr, fl, ls, lxr, lyr, lc, oys, oyr, oxs, oxr, ofs, ofr, ors):
    head, blk = lax.axis_index("head"), lax.axis_index("blk")
    x, y_lo, z = blk % 4, (blk // 4) % 2, blk // 8
    core = head % 2
    y = (head // 2) * 2 + y_lo
    mine = (y + 7 - x) % 4
    active = mine < 3
    own_row = core == y_lo

    def device(dx, dy, dz, dc):
        return {"head": (dy // 2) * 2 + dc, "blk": dz * 8 + (dy % 2) * 4 + dx}

    def remote(src, dst, send, recv, to):
        return pltpu.make_async_remote_copy(
            src_ref=src, dst_ref=dst, send_sem=send, recv_sem=recv, device_id=to, device_id_type=MESH
        )

    def wait(ref, sem):
        pltpu.make_async_copy(ref, ref, sem).wait()

    def either(local, src, dst, send, recv, to):
        @pl.when(local)
        def _():
            pltpu.make_async_copy(src, dst, recv).start()

        @pl.when(jnp.logical_not(local))
        def _():
            remote(src, dst, send, recv, to).start()

    barrier = pltpu.get_barrier_semaphore()
    for d in range(1, 4):
        for c in range(2):
            pl.semaphore_signal(barrier, inc=1, device_id=device((x + d) % 4, y, z, c), device_id_type=MESH)
            pl.semaphore_signal(barrier, inc=1, device_id=device(x, (y + d) % 4, z, c), device_id_type=MESH)
    pl.semaphore_signal(barrier, inc=1, device_id=device(x, y, z, 1 - core), device_id_type=MESH)
    across = device(x, y, (z + 2 * core + 3) % 4, 1 - core)
    pl.semaphore_signal(barrier, inc=1, device_id=across, device_id_type=MESH)
    pl.semaphore_wait(barrier, 14)

    arrays = (
        (k_hbm, relay_k, near_k, 0, 2),
        (v_hbm, relay_v, near_v, 0, 2),
        (q_hbm, relay_q, win_q, 0, 1),
        (q_hbm, relay_p, win_q, 1, 1),
    )

    def turn(i, row):
        late = (x // 2 + row) % 2
        return jnp.where(
            i == 3, x, jnp.where(i == 2 * (1 - late), x + 1 - 2 * (x % 2), 2 * (1 - x // 2) + (x + 3 + i - late) % 2)
        )

    def along_x(a):
        src, relay, _, tile, count = arrays[a]
        for d in (2, 1, 3):
            to = (x + d) % 4
            columns = pl.ds(pl.multiple_of(to * GROUP, GROUP), GROUP)
            block = src.at[pl.ds(tile, count), :, columns]
            remote(block, relay.at[x], xs.at[a], xr.at[a, d], device(to, y, z, core)).start()

    def then_along_y(a, start, first):
        src, relay, window, tile, count = arrays[a]
        base = tile if a >= 2 else 16 * y_lo
        if not first:
            wait(relay.at[start], xr.at[a, (x + 4 - start) % 4])

        def one(j, carry):
            to = (x + 1 + j) % 4
            if first:
                block = src.at[pl.ds(tile, count), :, pl.ds(pl.multiple_of((3 * x + j) * HD, HD), HD)]
            else:
                block = relay.at[start, :, :, pl.ds(pl.multiple_of(j * HD, HD), HD)]
            place = window.at[pl.ds(base + start * 8 + head * 2, count)]
            either(own_row & (to == y), block, place, ys.at[a], yr.at[min(a, 2), start], device(x, to, z, y_lo))
            return carry

        lax.fori_loop(0, 3, one, 0)

    def others_along_y(a, i):
        start = turn(i, y_lo)

        @pl.when(start != x)
        def _():
            then_along_y(a, start, False)

    def along_y(a):
        src, relay, _, tile, count = arrays[a]
        for d in (2, 1, 3):
            to = (y + d) % 4

            def one(k, carry):
                column = (to + 1 + k) % 4
                columns = pl.ds(pl.multiple_of((3 * column + 2 - k) * HD, HD), HD)
                block = src.at[pl.ds(tile, count), :, columns]
                remote(block, relay.at[y, k], xs.at[a], xr.at[a, d], device(x, to, z, core)).start()
                return carry

            lax.fori_loop(0, 3, one, 0)

    def then_along_x(a, d):
        src, relay, window, tile, count = arrays[a]
        source = (y + 4 - d) % 4
        base = tile if a >= 2 else 16 * (source % 2)
        if d:
            wait(relay.at[source, pl.ds(0, 3)], xr.at[a, d])

        def one(k, carry):
            to = (y + 1 + k) % 4
            if d:
                block = relay.at[source, k]
            else:
                block = src.at[pl.ds(tile, count), :, pl.ds(pl.multiple_of((3 * to + 2 - k) * HD, HD), HD)]
            peer = (source // 2) * 2 + core
            place = window.at[pl.ds(base + x * 8 + peer * 2, count)]
            local = (to == x) & (source % 2 == core)
            either(local, block, place, ys.at[a], yr.at[min(a, 2), x], device(to, y, z, source % 2))
            return carry

        lax.fori_loop(0, 3, one, 0)

    sibling = device(x, y, z, 1 - core)

    def forward(a, start):
        near, far = ((near_k, far_k), (near_v, far_v))[a]
        block = near.at[pl.ds(16 * core + start * 8, 8)]
        wait(block, yr.at[a, start])

        @pl.when(start // 2 == core)
        def _():
            place = far.at[pl.ds(32 * (1 - core) + (start % 2) * 8, 8)]
            remote(block, place, fs.at[a], fr.at[a, 1], across).start()

        @pl.when(start // 2 != core)
        def _():
            place = near.at[pl.ds(32 * core + (start % 2) * 8, 8)]
            remote(block, place, fs.at[a], fr.at[a, 0], sibling).start()

        pltpu.make_async_copy(block, far.at[pl.ds(16 * (1 - core) + start * 8, 8)], fl.at[a]).start()

    for d in range(1, 4):
        remote(lists_hbm, lists_r.at[x], ls, lxr.at[d], device((x + d) % 4, y, z, core)).start()
    own_lists = pltpu.make_async_copy(lists_hbm, lists_r.at[x], lc.at[0])
    own_lists.start()

    along_x(0)
    along_y(1)
    then_along_y(0, x, True)
    then_along_x(1, 0)
    for i, d in ((2, 2), (1, 1), (0, 3)):
        others_along_y(0, i)
        then_along_x(1, d)

    own_lists.wait()
    for d in range(1, 4):
        wait(lists_r.at[x], lxr.at[d])

    @pl.when(head == 0)
    def _():
        for j in range(3):
            to = (x + 1 + j) % 4
            either(own_row & (to == y), lists_r, lists_v, ls, lyr, device(x, to, z, y_lo))

    @pl.when(active)
    def _():
        for i in (3, 2):
            for a in range(2):
                forward(a, turn(i, core))

    along_x(2)
    along_y(3)
    then_along_y(2, x, True)
    then_along_x(3, 0)

    @pl.when(active)
    def _():
        for i in (1, 0):
            for a in range(2):
                forward(a, turn(i, core))

    for i, d in ((0, 2), (1, 1), (2, 3)):
        others_along_y(2, i)
        then_along_x(3, d)

    def out_x(i):
        to = turn(i, y_lo)

        @pl.when(to != x)
        def _():
            wait(relay_o.at[to], oyr.at[(x + 4 - to) % 4])
            columns = pl.ds(pl.multiple_of(x * GROUP, GROUP), GROUP)
            remote(relay_o.at[to], out_hbm.at[pl.ds(0, 1), :, columns], oxs, oxr, device(to, y, z, core)).start()

    def out_y(i):
        for k in range(1, 4):
            start = (x + k) % 4
            late = (start // 2 + core) % 2
            theirs = jnp.where(x // 2 == start // 2, 2 * (1 - late), (x + start + 1) % 2 + late)

            @pl.when((start != y) & (theirs == i))
            def _():
                wait(relay_r.at[start], ofr.at[start])
                column = 3 * start + (y + 7 - start) % 4

                def one(peer, carry):
                    block = relay_r.at[start, pl.ds(peer, 1)]
                    place = out_hbm.at[pl.ds(1, 1), :, pl.ds(pl.multiple_of(column * HD, HD), HD)]
                    to = {"head": peer, "blk": z * 8 + core * 4 + x}
                    either(own_row & (peer == head), block, place, ors, oxr, to)
                    return carry

                lax.fori_loop(0, 4, one, 0)

    @pl.when(active)
    def _():
        wait(lists_v, lyr)
        for i in range(4):
            place = (lists_v[i] + (272 - ROW * (2 * z + core) - 16 * (i // 2))) & 255
            lists_w[i] = jnp.minimum(place, ROW + 15)
        to_scalar = pltpu.make_async_copy(lists_w, lists_s, lc.at[1])
        to_scalar.start()
        for a in range(2):
            wait(near_k.at[pl.ds(0, 16)], fr.at[a, 0])
        to_scalar.wait()

        def attend(start, keys_ref, values_ref):
            spots = [[lists_s[start, t, e] for e in range(SEL)] for t in range(8)]

            def scores_of(t):
                keys = jnp.concatenate([keys_ref[w] for w in spots[t]], axis=0)
                query = win_q[start * 8 + t]
                return lax.dot_general(query, keys, (((1,), (1,)), ((), ())), preferred_element_type=jnp.float32)

            later = scores_of(0)
            for t in range(8):
                scores = later
                if t < 7:
                    later = scores_of(t + 1)
                peak = jnp.max(scores, axis=1, keepdims=True)
                weights = jnp.exp2((scores - peak) * EXP2)
                total = jnp.sum(weights, axis=1, keepdims=True)
                values = jnp.concatenate([values_ref[w] for w in spots[t]], axis=0)
                mixed = jnp.dot(weights.astype(jnp.bfloat16), values, preferred_element_type=jnp.float32)
                win_o[t % 2, start * 4 + t // 2] = (mixed / total).astype(jnp.bfloat16)

        def quarter(i, carry):
            start = turn(i, core)
            wait(win_q.at[pl.ds(start * 8, 8)], yr.at[2, start])

            @pl.when(start // 2 != core)
            def _():
                attend(start, near_k, near_v)

            @pl.when((start // 2 == core) & (i == 2 - (x // 2 + core) % 2))
            def _():
                for a in range(2):
                    wait(far_k.at[pl.ds(0, 16)], fr.at[a, 1])
                    wait(far_k.at[pl.ds(0, 32)], fl.at[a])

            @pl.when(start // 2 == core)
            def _():
                attend(start, far_k, far_v)

            @pl.when(start != x)
            def _():
                block = win_o.at[1, pl.ds(start * 4, 4)]
                remote(block, relay_r.at[x], ofs, ofr.at[x], device(start, y, z, core)).start()

            def send(peer, carry):
                to = {"head": peer, "blk": z * 8 + core * 4 + x}
                local = own_row & (peer == head)

                @pl.when(start != x)
                def _():
                    block = win_o.at[0, pl.ds(start * 4 + peer, 1)]
                    place = relay_o.at[start, :, :, pl.ds(pl.multiple_of(mine * HD, HD), HD)]
                    either(local, block, place, oys, oyr.at[(x + 4 - start) % 4], to)

                @pl.when(start == x)
                def _():
                    block = win_o.at[:, start * 4 + peer]
                    place = out_hbm.at[:, :, pl.ds(pl.multiple_of((3 * x + mine) * HD, HD), HD)]
                    either(local, block, place, oys, oxr, to)

                return carry

            lax.fori_loop(0, 4, send, 0)
            return carry

        lax.fori_loop(0, 4, quarter, 0)
        for i in range(4):
            out_x(i)
            out_y(i)

    @pl.when(jnp.logical_not(active))
    def _():
        for i in range(4):
            out_x(i)
            out_y(i)

    wait(out_hbm, oxr)
    wait(relay_o.at[pl.ds(0, 3)], oxs)
    for d in range(3):
        wait(lists_r.at[x], ls)
    wait(relay_k.at[pl.ds(0, 3)], xs.at[0])
    wait(relay_v.at[pl.ds(0, 3), pl.ds(0, 3)], xs.at[1])
    wait(relay_q.at[pl.ds(0, 3)], xs.at[2])
    wait(relay_p.at[pl.ds(0, 3), pl.ds(0, 3)], xs.at[3])
    itself = own_row & active

    @pl.when(itself)
    def _():
        wait(win_q.at[pl.ds(0, 16)], ys.at[0])
        wait(win_q.at[pl.ds(0, 8)], ys.at[2])
        wait(win_q.at[pl.ds(0, 15)], oys)

    @pl.when(jnp.logical_not(itself))
    def _():
        wait(win_q.at[pl.ds(0, 24)], ys.at[0])
        wait(win_q.at[pl.ds(0, 12)], ys.at[2])

    @pl.when(active)
    def _():
        wait(win_q.at[pl.ds(0, 20)], ys.at[1])
        wait(win_q.at[pl.ds(0, 10)], ys.at[3])

    @pl.when(jnp.logical_not(active))
    def _():
        wait(win_q.at[pl.ds(0, 24)], ys.at[1])
        wait(win_q.at[pl.ds(0, 12)], ys.at[3])

    for idle, own, count in ((0, 0, 8), (0, 1, 6), (1, 0, 12), (1, 1, 9)):

        @pl.when((active if not idle else jnp.logical_not(active)) & (own_row if own else jnp.logical_not(own_row)))
        def _():
            wait(win_q.at[pl.ds(0, count)], ors)

    @pl.when(active & jnp.logical_not(own_row))
    def _():
        wait(win_q.at[pl.ds(0, 20)], oys)

    @pl.when(active)
    def _():
        wait(win_q.at[pl.ds(0, 12)], ofs)
        for a in range(2):
            wait(win_q, fs.at[a])

    @pl.when(head == 0)
    def _():
        for j in range(2):
            wait(lists_v, ls)

        @pl.when(jnp.logical_not(itself))
        def _():
            wait(lists_v, ls)


def local(queries, key_rows, value_rows, tile_lists):
    bf16, dma = jnp.bfloat16, pltpu.SemaphoreType.DMA
    relay = pltpu.VMEM((4, 2, TILE, GROUP), bf16)
    window = pltpu.VMEM((ROW + 16, TILE, HD), bf16)
    lists = pltpu.VMEM((4, 8, SEL), jnp.int32)
    tiles = (2, TILE, queries.shape[1])
    result = pl.pallas_call(
        kernel,
        out_shape=jax.ShapeDtypeStruct(tiles, bf16),
        in_specs=[pl.BlockSpec(memory_space=pl.ANY)] * 4,
        out_specs=pl.BlockSpec(memory_space=pl.ANY),
        scratch_shapes=[
            relay, pltpu.VMEM((4, 3, 2, TILE, HD), bf16),
            pltpu.VMEM((4, 1, TILE, GROUP), bf16), pltpu.VMEM((4, 3, 1, TILE, HD), bf16),
            pltpu.VMEM((4, 1, TILE, GROUP), bf16), pltpu.VMEM((4, 4, TILE, HD), bf16),
            window, window, window, window,
            pltpu.VMEM((ROW, TILE, HD), bf16), pltpu.VMEM((2, ROW // 2, TILE, HD), bf16),
            lists, lists, lists, pltpu.SMEM((4, 8, SEL), jnp.int32),
            dma((4,)), dma((4, 4)), dma((4,)), dma((3, 4)), dma((2,)), dma((2, 2)), dma((2,)),
            dma, dma((4,)), dma, dma((2,)), dma, dma((4,)), dma, dma, dma, dma((4,)), dma,
        ],
        compiler_params=pltpu.CompilerParams(collective_id=0, has_side_effects=True, vmem_limit_bytes=56 * 2**20),
        cost_estimate=pl.CostEstimate(flops=4 * 10**9, bytes_accessed=8 * 10**6, transcendentals=8 * 10**6),
    )(queries.reshape(tiles), key_rows.reshape(tiles), value_rows.reshape(tiles), tile_lists)
    return result.reshape(queries.shape)


def solution(mesh):
    tokens = P(("blk", "head"), None)
    return jax.shard_map(
        local, mesh=mesh, in_specs=(tokens, tokens, tokens, P("blk", None)), out_specs=tokens, check_vma=False
    )
```
